1024 devices in a mesh: section: 64 (over z, x_hi), dp: 16 (over y, x_lo, core).
Axes of the slice: x: 4 (x_hi: 2, x_lo: 2; x = x_hi * 2 + x_lo), y: 4, z: 32, core: 2. Of those that a mesh axis runs over, the one named last changes fastest.
Arguments:
- fwd_hidden: bfloat16 [64, 16, 64, 2048], P('section', 'dp'), may hold values from -6 to 6
- fwd_query: bfloat16 [64, 16, 64, 2048], P('section', 'dp'), may hold values from -32 to 32
- bwd_hidden: bfloat16 [64, 16, 64, 2048], P('section', 'dp'), may hold values from -6 to 6
- bwd_query: bfloat16 [64, 16, 64, 2048], P('section', 'dp'), may hold values from -32 to 32
- bwd_grad: bfloat16 [64, 16, 64, 2048], P('section', 'dp'), may hold values from -6 to 6
- prefix_keys: bfloat16 [64, 16, 2, 128, 512], P('section', 'dp'), may hold values from -6 to 6
- prefix_values: bfloat16 [64, 16, 2, 128, 512], P('section', 'dp'), may hold values from -6 to 6
- key_weight: bfloat16 [64, 2048, 512], P('section'), may hold values from -0.125 to 0.125
- value_weight: bfloat16 [64, 2048, 512], P('section'), may hold values from -0.125 to 0.125
- block_ids: int32 [64, 16, 2, 1], P('section', 'dp'), may hold values from 0 to 1, as said below
Outputs:
- next_hidden: bfloat16 [64, 16, 64, 2048], P('section', 'dp')
- prev_grad: bfloat16 [64, 16, 64, 2048], P('section', 'dp')
- query_grad: bfloat16 [64, 16, 64, 2048], P('section', 'dp')
- prefix_key_grad: bfloat16 [64, 16, 1, 128, 512], P('section', 'dp')
- prefix_value_grad: bfloat16 [64, 16, 1, 128, 512], P('section', 'dp')
- key_weight_grad: bfloat16 [64, 2048, 512], P('section', 'dp')
- value_weight_grad: bfloat16 [64, 2048, 512], P('section', 'dp')
The draws below stay inside these ranges and needn't reach their ends.
Inputs may be any that keep to these rules, and one draw needn't show every extreme that they name: `block_ids`: the 1 indices of one group's list are distinct.
All inputs are finite; a program needn't handle non-finite values.
Results may differ from the reference program's by a relative error of at most 0.025.
Values may be sent and summed in bfloat16 or wider, within the bound.
No kernel may reach another device: no remote copies, remote signals or barrier semaphores. Data moves between devices by JAX's collectives and lax.ppermute only.
A program may use at most 64 MiB of HBM per device.

```python
import jax
import jax.numpy as jnp
from jax import lax

HEADS = 16
KVH = 4
HD = 128
D = 2048
CH = 64
BLK = 128
NBLK = 1
POOL = 2
SECTIONS = 64
REPL = 16


def query_draw(key, salt):
    dims_all = (SECTIONS, REPL, CH, HEADS * HD)
    local_key = jax.random.fold_in(key, salt)
    values = jnp.clip(jax.random.normal(local_key, dims_all, jnp.float32), -6.0, 6.0)
    return values.astype(jnp.bfloat16)


def draw_fwd_query(key, part):
    return query_draw(key, 101)


def draw_bwd_query(key, part):
    return query_draw(key, 202)


def draw_prefix_keys(key, part):
    dims_all = (SECTIONS, REPL, POOL, BLK, KVH * HD)
    local_key = jax.random.fold_in(key, 303)
    values = jnp.clip(jax.random.normal(local_key, dims_all, jnp.float32), -6.0, 6.0)
    return values.astype(jnp.bfloat16)


def pick_blocks(one_key):
    return jax.random.permutation(one_key, POOL)[:NBLK]


def draw_block_ids(key, part):
    total_lists = SECTIONS * REPL * 2
    keys_all = jax.random.split(jax.random.fold_in(key, 404), total_lists)
    picks = jax.vmap(pick_blocks)(keys_all)
    return picks.reshape(SECTIONS, REPL, 2, NBLK).astype(jnp.int32)


def with_spikes(array, key, source, target, shards_of, factor):
    def block_of(axis_at):
        return (jnp.arange(array.shape[axis_at]) // (array.shape[axis_at] // shards_of)).reshape((-1,) + (1,) * (array.ndim - 1 - axis_at))

    first = jax.random.permutation(key, shards_of)[block_of(target)]
    far = (block_of(target) + shards_of // 2) % shards_of
    return jnp.where((block_of(source) == first) | (block_of(source) == far), factor * array, array)


def shard_levels(key, shape, pieces, low, top_value):
    loudness = 1.0
    for dim, parts in pieces:
        steps = jax.random.uniform(jax.random.fold_in(jax.random.fold_in(key, 6), dim), (parts,), jnp.float32, low / len(pieces), top_value / len(pieces))
        loudness = loudness * jnp.repeat(jnp.exp(steps), shape[dim] // parts).reshape((-1,) + (1,) * (len(shape) - 1 - dim))
    return loudness


def bell_draw(own_key, shape, scale, bound, pieces=(), held_as=jnp.bfloat16):
    loudness = shard_levels(own_key, shape, pieces, -0.22, 0.18) if pieces else 1.0
    values = jax.random.normal(own_key, shape, jnp.float32) * scale * loudness
    return jnp.minimum(jnp.maximum(values, -bound), bound).astype(held_as)


def heavy_noise(key, extent, scale, bound, pieces, heavy, kind=jnp.bfloat16):
    values = scale * jax.random.normal(key, extent, jnp.float32)
    if pieces:
        values = values * shard_levels(key, extent, pieces, -0.22, 0.18)
    return jnp.clip(with_spikes(values, jax.random.fold_in(key, 3), *heavy), -bound, bound).astype(kind)


def setup_inputs(seed: int = 0) -> dict:
    arg_keys = jax.random.split(jax.random.key(seed), 11)
    return {
        "fwd_hidden": bell_draw(arg_keys[0], (SECTIONS, REPL, CH, D), 1.0, 6.0, ((0, 64), (1, 16))),
        "fwd_query": draw_fwd_query(jax.random.fold_in(arg_keys[10], 71), 0),
        "bwd_hidden": heavy_noise(arg_keys[2], (SECTIONS, REPL, CH, D), 1.0, 6.0, ((0, 64), (1, 16)), (1, 3, 16, 2.0)),
        "bwd_query": draw_bwd_query(jax.random.fold_in(arg_keys[10], 71), 0),
        "bwd_grad": bell_draw(arg_keys[4], (SECTIONS, REPL, CH, D), 1.0, 6.0, ((0, 64), (1, 16))),
        "prefix_keys": draw_prefix_keys(jax.random.fold_in(arg_keys[10], 71), 0),
        "prefix_values": bell_draw(arg_keys[6], (SECTIONS, REPL, POOL, BLK, KVH * HD), 1.0, 6.0, ((0, 64), (1, 16))),
        "key_weight": bell_draw(arg_keys[7], (SECTIONS, D, KVH * HD), D ** -0.5, 0.125, ((0, 64),)),
        "value_weight": bell_draw(arg_keys[8], (SECTIONS, D, KVH * HD), D ** -0.5, 0.125, ((0, 64),)),
        "block_ids": draw_block_ids(jax.random.fold_in(arg_keys[10], 71), 0),
    }


def kv_heads(hidden, weight_k, weight_v):
    keys_new = jnp.dot(hidden, weight_k, preferred_element_type=jnp.float32).astype(jnp.bfloat16)
    values_new = jnp.dot(hidden, weight_v, preferred_element_type=jnp.float32).astype(jnp.bfloat16)
    return keys_new, values_new


def gather_context(hidden, chosen_row, pool_keys, pool_values, weight_k, weight_v):
    keys_new, values_new = kv_heads(hidden, weight_k, weight_v)
    kv_width = pool_keys.shape[-1]
    prefix_keys_sel = jnp.take(pool_keys, chosen_row, axis=0).reshape(-1, kv_width)
    prefix_values_sel = jnp.take(pool_values, chosen_row, axis=0).reshape(-1, kv_width)
    keys_all = jnp.concatenate([prefix_keys_sel, keys_new], axis=0)
    values_all = jnp.concatenate([prefix_values_sel, values_new], axis=0)
    return keys_all, values_all


def softmax_probs(query_rows, keys_all, prefix_rows):
    row_count = query_rows.shape[0]
    key_count = keys_all.shape[0]
    query_heads = query_rows.astype(jnp.float32).reshape(row_count, KVH, HEADS // KVH, HD)
    key_heads = keys_all.astype(jnp.float32).reshape(key_count, KVH, HD)
    scores = jnp.einsum("cgqd,kgd->gqck", query_heads, key_heads) * (HD ** -0.5)
    row_pos = jnp.arange(row_count)[:, None]
    col_pos = jnp.arange(key_count)[None, :]
    visible = (col_pos < prefix_rows) | (col_pos - prefix_rows <= row_pos)
    scores = jnp.where(visible, scores, -jnp.inf)
    highest = jnp.max(scores, axis=-1, keepdims=True)
    raised = jnp.exp(scores - highest)
    return raised / jnp.sum(raised, axis=-1, keepdims=True)


def one_site(hidden_fwd, query_fwd, hidden_bwd, query_bwd, grad_out, pool_keys, pool_values, weight_k, weight_v, chosen):
    row_count = hidden_fwd.shape[0]
    kv_width = pool_keys.shape[-1]
    prefix_rows = NBLK * BLK
    keys_fwd, values_fwd = gather_context(hidden_fwd, chosen[0], pool_keys, pool_values, weight_k, weight_v)
    key_count = keys_fwd.shape[0]
    probs_fwd = softmax_probs(query_fwd, keys_fwd, prefix_rows)
    value_heads_fwd = values_fwd.astype(jnp.float32).reshape(key_count, KVH, HD)
    attended = jnp.einsum("gqck,kgd->cgqd", probs_fwd.astype(jnp.bfloat16).astype(jnp.float32), value_heads_fwd).reshape(row_count, -1)
    out_fwd = (hidden_fwd.astype(jnp.float32) + attended).astype(jnp.bfloat16)

    keys_bwd, values_bwd = gather_context(hidden_bwd, chosen[1], pool_keys, pool_values, weight_k, weight_v)
    probs_bwd = softmax_probs(query_bwd, keys_bwd, prefix_rows)
    weights_bwd = probs_bwd.astype(jnp.bfloat16).astype(jnp.float32)
    grad_heads = grad_out.astype(jnp.float32).reshape(row_count, KVH, HEADS // KVH, HD)
    key_heads = keys_bwd.astype(jnp.float32).reshape(key_count, KVH, HD)
    value_heads = values_bwd.astype(jnp.float32).reshape(key_count, KVH, HD)
    query_heads = query_bwd.astype(jnp.float32).reshape(row_count, KVH, HEADS // KVH, HD)
    grad_probs = jnp.einsum("cgqd,kgd->gqck", grad_heads, value_heads)
    inner_sum = jnp.sum(probs_bwd * grad_probs, axis=-1, keepdims=True)
    grad_scores = (probs_bwd * (grad_probs - inner_sum) * (HD ** -0.5)).astype(jnp.bfloat16).astype(jnp.float32)
    query_grad = jnp.einsum("gqck,kgd->cgqd", grad_scores, key_heads).reshape(row_count, -1).astype(jnp.bfloat16)
    key_grads = jnp.einsum("gqck,cgqd->kgd", grad_scores, query_heads).reshape(key_count, kv_width)
    value_grads = jnp.einsum("gqck,cgqd->kgd", weights_bwd, grad_heads).reshape(key_count, kv_width)
    prefix_key_grad = key_grads[:prefix_rows].astype(jnp.bfloat16).reshape(NBLK, BLK, kv_width)
    prefix_value_grad = value_grads[:prefix_rows].astype(jnp.bfloat16).reshape(NBLK, BLK, kv_width)
    own_keys = key_grads[prefix_rows:].astype(jnp.bfloat16)
    own_values = value_grads[prefix_rows:].astype(jnp.bfloat16)
    grad_back = grad_out.astype(jnp.float32) + jnp.dot(own_keys, weight_k.T, preferred_element_type=jnp.float32) + jnp.dot(own_values, weight_v.T, preferred_element_type=jnp.float32)
    own_grads = jnp.concatenate([own_keys, own_values], axis=1)
    partial_grad = jnp.dot(hidden_bwd.T, own_grads, preferred_element_type=jnp.float32).astype(jnp.bfloat16)
    return out_fwd, grad_back.astype(jnp.bfloat16), query_grad, prefix_key_grad, prefix_value_grad, partial_grad


def reference(fwd_hidden, fwd_query, bwd_hidden, bwd_query, bwd_grad, prefix_keys, prefix_values, key_weight, value_weight, block_ids):
    def per_section(items):
        weight_k = items[7]
        weight_v = items[8]

        def per_replica(hidden_fwd, query_fwd, hidden_bwd, query_bwd, grad_out, pool_keys, pool_values, chosen):
            return one_site(hidden_fwd, query_fwd, hidden_bwd, query_bwd, grad_out, pool_keys, pool_values, weight_k, weight_v, chosen)

        results = jax.vmap(per_replica)(items[0], items[1], items[2], items[3], items[4], items[5], items[6], items[9])
        partial_grad = lax.optimization_barrier(results[5])
        summed = jnp.sum(partial_grad.astype(jnp.float32), axis=0)
        return results[0], results[1], results[2], results[3], results[4], summed

    out_fwd, grad_back, query_grad, prefix_key_grad, prefix_value_grad, summed = lax.map(
        per_section, (fwd_hidden, fwd_query, bwd_hidden, bwd_query, bwd_grad, prefix_keys, prefix_values, key_weight, value_weight, block_ids))
    next_hidden = jnp.roll(out_fwd, 1, axis=0)
    prev_grad = jnp.concatenate([grad_back[1:], jnp.zeros_like(grad_back[:1])], axis=0)
    kv_width = KVH * HD
    key_weight_grad = summed[:, :, :kv_width].astype(jnp.bfloat16)
    value_weight_grad = summed[:, :, kv_width:].astype(jnp.bfloat16)
    return (next_hidden, prev_grad, query_grad, prefix_key_grad, prefix_value_grad, key_weight_grad, value_weight_grad)
```

```python
import functools

import jax
import jax.numpy as jnp
from jax import lax
from jax.experimental import pallas as pl
from jax.experimental.pallas import tpu as pltpu
from jax.sharding import PartitionSpec as P

HEADS = 16
KVH = 4
HD = 128
GROUP = HEADS // KVH
D = 2048
CH = 64
BLK = 128
KVW = KVH * HD
KEYS = BLK + CH
SCALE = HD ** (-0.5)
CHIPS = 8
ROWS = D // CHIPS
HALF = ROWS // 2
CHUNKS = 4
STEP = D // CHUNKS
F32 = jnp.float32
BF16 = jnp.bfloat16

VMEM = pltpu.VMEM
ANY = pl.ANY
SMEM = pltpu.SMEM


def nt(a, b):
    return lax.dot_general(a, b, (((1,), (1,)), ((), ())), preferred_element_type=F32)


def nn(a, b):
    return lax.dot_general(a, b, (((1,), (0,)), ((), ())), preferred_element_type=F32)


def tn(a, b):
    return lax.dot_general(a, b, (((0,), (0,)), ((), ())), preferred_element_type=F32)


def stacked(ref, g):
    return jnp.concatenate(
        [ref[:, (g * GROUP + j) * HD : (g * GROUP + j + 1) * HD] for j in range(GROUP)], axis=0
    )


def probs_t(keys, query):
    score = nt(keys, query) * SCALE
    key_at = lax.broadcasted_iota(jnp.int32, (CH, GROUP * CH), 0)
    row_at = lax.broadcasted_iota(jnp.int32, (CH, GROUP * CH), 1) % CH
    own = jnp.where(key_at <= row_at, score[BLK:], -jnp.inf)
    score = jnp.concatenate([score[:BLK], own], axis=0)
    raised = jnp.exp(score - jnp.max(score, axis=0, keepdims=True))
    return raised * (1.0 / jnp.sum(raised, axis=0, keepdims=True))


def project(hid, weight, parts, wait):
    total = None
    for c in parts:
        wait(c)
        part = nn(hid[:, c * STEP : (c + 1) * STEP], weight[c * STEP : (c + 1) * STEP, :])
        total = part if total is None else total + part
    return total.astype(BF16)


def backward_kernel(
    ids, hid_h, q_h, g_h, pk_h, pv_h, wk_h, wv_h,
    send_h, own_h, pkg_h, pvg_h, gs_h, keys_h,
    hid, q, g, keys, values, wk, wv, own, pkg, pvg, gs, sem, wsem, osem,
):
    block = ids[1]
    load = [
        pltpu.make_async_copy(hid_h, hid, sem.at[0]),
        pltpu.make_async_copy(q_h, q, sem.at[1]),
        pltpu.make_async_copy(pk_h.at[block], keys.at[pl.ds(0, BLK)], sem.at[2]),
        pltpu.make_async_copy(g_h, g, sem.at[3]),
        pltpu.make_async_copy(pv_h.at[block], values.at[pl.ds(0, BLK)], sem.at[4]),
    ]
    wload = []
    for i, (src, dst) in enumerate(((wk_h, wk), (wv_h, wv))):
        for c in range(CHUNKS):
            at = pl.ds(c * STEP, STEP)
            wload.append(pltpu.make_async_copy(src.at[at], dst.at[at], wsem.at[i * CHUNKS + c]))
    load[0].start()
    for copy in wload[:CHUNKS]:
        copy.start()
    for copy in load[1:3]:
        copy.start()
    for copy in wload[CHUNKS:]:
        copy.start()
    for copy in load[3:]:
        copy.start()
    load[0].wait()
    out = []

    def put(src, dst):
        copy = pltpu.make_async_copy(src, dst, osem.at[len(out)])
        copy.start()
        out.append(copy)

    for t in range(CHIPS):
        put(hid.at[:, pl.ds(t * ROWS, ROWS)], send_h.at[t, :, pl.ds(0, ROWS)])
    keys[BLK:, :] = project(hid, wk, range(CHUNKS), lambda c: wload[c].wait())
    values[BLK:, :] = project(hid, wv, range(CHUNKS), lambda c: wload[CHUNKS + c].wait())
    for copy in load[1:]:
        copy.wait()
    put(keys, keys_h)
    for h in range(KVH):
        at = slice(h * HD, (h + 1) * HD)
        query, grad = stacked(q, h), stacked(g, h)
        probs = probs_t(keys[:, at], query)
        grad_probs = nt(values[:, at], grad)
        inner = jnp.sum(probs * grad_probs, axis=0, keepdims=True)
        grad_scores = (probs * (grad_probs - inner) * SCALE).astype(BF16)
        gs[h] = grad_scores
        key_grads = nn(grad_scores, query)
        value_grads = nn(probs.astype(BF16), grad)
        own[:, at] = key_grads[BLK:].astype(BF16)
        own[:, KVW + h * HD : KVW + (h + 1) * HD] = value_grads[BLK:].astype(BF16)
        pkg[:, at] = key_grads[:BLK].astype(BF16)
        pvg[:, at] = value_grads[:BLK].astype(BF16)
    for t in range(CHIPS):
        put(own, send_h.at[t, :, pl.ds(ROWS, 2 * KVW)])
    put(own, own_h)
    put(pkg, pkg_h)
    put(pvg, pvg_h)
    put(gs, gs_h)
    for copy in out:
        copy.wait()


def forward_kernel(
    ids, hid_h, q_h, pk_h, pv_h, wk_h, wv_h, g_h, own_h,
    fwd_h, back_h,
    hid, q, keys, values, wk, wv, g, own, fwd, back, sem, wsem, osem,
):
    block = ids[0]
    load = [
        pltpu.make_async_copy(g_h, g, sem.at[0]),
        pltpu.make_async_copy(own_h, own, sem.at[1]),
        pltpu.make_async_copy(hid_h, hid, sem.at[2]),
        pltpu.make_async_copy(q_h, q, sem.at[3]),
        pltpu.make_async_copy(pk_h.at[block], keys.at[pl.ds(0, BLK)], sem.at[4]),
        pltpu.make_async_copy(pv_h.at[block], values.at[pl.ds(0, BLK)], sem.at[5]),
    ]
    wload = []
    for i, (src, dst) in enumerate(((wk_h, wk), (wv_h, wv))):
        for c in range(CHUNKS):
            at = pl.ds(c * STEP, STEP)
            wload.append(pltpu.make_async_copy(src.at[at], dst.at[at], wsem.at[i * CHUNKS + c]))
    for copy in load[:3]:
        copy.start()
    for c in range(CHUNKS):
        wload[c].start()
        wload[CHUNKS + c].start()
    for copy in load[3:]:
        copy.start()
    for copy in load[:3]:
        copy.wait()
    key_total = value_total = None
    for c in range(CHUNKS):
        at = slice(c * STEP, (c + 1) * STEP)
        wload[c].wait()
        wload[CHUNKS + c].wait()
        back[:, at] = (
            g[:, at].astype(F32)
            + nt(own[:, :KVW], wk[at, :])
            + nt(own[:, KVW:], wv[at, :])
        ).astype(BF16)
        key_part = nn(hid[:, at], wk[at, :])
        value_part = nn(hid[:, at], wv[at, :])
        key_total = key_part if c == 0 else key_total + key_part
        value_total = value_part if c == 0 else value_total + value_part
    back_out = pltpu.make_async_copy(back, back_h, osem.at[0])
    back_out.start()
    keys[BLK:, :] = key_total.astype(BF16)
    values[BLK:, :] = value_total.astype(BF16)
    for copy in load[3:]:
        copy.wait()
    for h in range(KVH):
        at = slice(h * HD, (h + 1) * HD)
        weights = probs_t(keys[:, at], stacked(q, h)).astype(BF16)
        attended = tn(weights, values[:, at])
        for j in range(GROUP):
            cols = slice((h * GROUP + j) * HD, (h * GROUP + j + 1) * HD)
            fwd[:, cols] = (
                hid[:, cols].astype(F32) + attended[j * CH : (j + 1) * CH]
            ).astype(BF16)
    fwd_out = pltpu.make_async_copy(fwd, fwd_h, osem.at[1])
    fwd_out.start()
    back_out.wait()
    fwd_out.wait()


def query_kernel(gs, keys, out):
    for h in range(KVH):
        grad = tn(gs[h], keys[:, h * HD : (h + 1) * HD])
        for j in range(GROUP):
            cols = slice((h * GROUP + j) * HD, (h * GROUP + j + 1) * HD)
            out[:, cols] = grad[j * CH : (j + 1) * CH].astype(BF16)


def weight_kernel(core, recv, mine, theirs):
    here = core[0]
    grads = recv[:, :, ROWS:].reshape(CHIPS * CH, 2 * KVW)
    low = tn(recv[:, :, :HALF].reshape(CHIPS * CH, HALF), grads)
    high = tn(recv[:, :, HALF:ROWS].reshape(CHIPS * CH, HALF), grads)
    first = here == 0
    mine[...] = jnp.where(first, low, high)
    theirs[...] = jnp.where(first, high, low).astype(BF16)


def sum_kernel(core, mine, both, key_grad, value_grad):
    other = both[1 - core[0]].astype(F32)
    key_grad[...] = (mine[:, :KVW] + other[:, :KVW]).astype(BF16)
    value_grad[...] = (mine[:, KVW:] + other[:, KVW:]).astype(BF16)


def call(kernel, outs, scratch, flops, in_specs, out_specs, size=62):
    return pl.pallas_call(
        kernel,
        out_shape=[jax.ShapeDtypeStruct(s, t) for s, t in outs],
        in_specs=in_specs,
        out_specs=out_specs,
        scratch_shapes=scratch,
        compiler_params=pltpu.CompilerParams(vmem_limit_bytes=size * 1024 * 1024),
        cost_estimate=pl.CostEstimate(flops=flops, bytes_accessed=6 << 20, transcendentals=200000),
    )


def spec(space):
    return pl.BlockSpec(memory_space=space)


def along(value, axis, steps, wrap):
    count = lax.axis_size(axis)
    pairs = [(i, (i + steps) % count) for i in range(count) if wrap or 0 <= i + steps < count]
    return lax.ppermute(value, axis, pairs)


def per_device(
    fwd_hidden, fwd_query, bwd_hidden, bwd_query, bwd_grad,
    prefix_keys, prefix_values, key_weight, value_weight, block_ids,
):
    count = lax.axis_size("dp")
    dma = pltpu.SemaphoreType.DMA
    wide, kv, weight = (CH, D), (KEYS, KVW), (D, KVW)
    pool_keys, pool_values = prefix_keys[0, 0], prefix_values[0, 0]
    weight_k, weight_v = key_weight[0], value_weight[0]
    grad = bwd_grad[0, 0]
    ids = block_ids.reshape(2)
    send, own, pkg, pvg, gs, keys_bwd = call(
        backward_kernel,
        [
            ((CHIPS, CH, ROWS + 2 * KVW), BF16),
            ((CH, 2 * KVW), BF16),
            ((BLK, KVW), BF16),
            ((BLK, KVW), BF16),
            ((KVH, KEYS, GROUP * CH), BF16),
            (kv, BF16),
        ],
        [VMEM(wide, BF16)] * 3
        + [VMEM(kv, BF16)] * 2
        + [VMEM(weight, BF16)] * 2
        + [VMEM((CH, 2 * KVW), BF16)]
        + [VMEM((BLK, KVW), BF16)] * 2
        + [VMEM((KVH, KEYS, GROUP * CH), BF16), dma((5,)), dma((2 * CHUNKS,)), dma((24,))],
        800_000_000,
        [spec(SMEM)] + [spec(ANY)] * 7,
        [spec(ANY)] * 6,
    )(ids, bwd_hidden[0, 0], bwd_query[0, 0], grad, pool_keys, pool_values, weight_k, weight_v)
    same_core = [[2 * t + c for t in range(count // 2)] for c in range(2)]
    pairs = [[2 * t, 2 * t + 1] for t in range(count // 2)]
    recv = lax.all_to_all(send, "dp", 0, 0, tiled=True, axis_index_groups=same_core)
    out_fwd, out_bwd = call(
        forward_kernel,
        [(wide, BF16), (wide, BF16)],
        [VMEM(wide, BF16)] * 2
        + [VMEM(kv, BF16)] * 2
        + [VMEM(weight, BF16)] * 2
        + [VMEM(wide, BF16), VMEM((CH, 2 * KVW), BF16)]
        + [VMEM(wide, BF16)] * 2
        + [dma((6,)), dma((2 * CHUNKS,)), dma((2,))],
        800_000_000,
        [spec(SMEM)] + [spec(ANY)] * 8,
        [spec(ANY)] * 2,
    )(
        ids, fwd_hidden[0, 0], fwd_query[0, 0], pool_keys, pool_values,
        weight_k, weight_v, grad, own,
    )
    next_hidden = along(out_fwd, "section", 1, True)
    prev_grad = along(out_bwd, "section", -1, False)
    (query_grad,) = call(
        query_kernel,
        [(wide, BF16)],
        [],
        100_000_000,
        [spec(VMEM)] * 2,
        [spec(VMEM)],
        16,
    )(gs, keys_bwd)
    core = lax.axis_index("dp") & 1
    mine, theirs = call(
        weight_kernel,
        [((HALF, 2 * KVW), F32), ((HALF, 2 * KVW), BF16)],
        [],
        270_000_000,
        [spec(SMEM), spec(VMEM)],
        [spec(VMEM)] * 2,
        16,
    )(core.reshape(1), recv)
    both = lax.all_gather(theirs, "dp", axis=0, axis_index_groups=pairs)
    key_weight_grad, value_weight_grad = call(
        sum_kernel,
        [((HALF, KVW), BF16)] * 2,
        [],
        1_000_000,
        [spec(SMEM)] + [spec(VMEM)] * 2,
        [spec(VMEM)] * 2,
        16,
    )(core.reshape(1), mine, both)
    return (
        next_hidden[None, None],
        prev_grad[None, None],
        query_grad[None, None],
        pkg[None, None, None],
        pvg[None, None, None],
        key_weight_grad[None],
        value_weight_grad[None],
    )


def solution(mesh):
    device = P("section", "dp")
    return jax.shard_map(
        per_device,
        mesh=mesh,
        in_specs=(device,) * 7 + (P("section"),) * 2 + (device,),
        out_specs=(device,) * 5 + (P("section", "dp"),) * 2,
        check_vma=False,
    )
```

```python
import functools

import jax
import jax.numpy as jnp
from jax import lax
from jax.experimental import pallas as pl
from jax.experimental.pallas import tpu as pltpu
from jax.sharding import PartitionSpec as P

HEADS = 16
KVH = 4
HD = 128
GROUP = HEADS // KVH
D = 2048
CH = 64
BLK = 128
KVW = KVH * HD
KEYS = BLK + CH
SCALE = HD ** (-0.5)
CHIPS = 8
ROWS = D // CHIPS
HALF = ROWS // 2
CHUNKS = 4
STEP = D // CHUNKS
F32 = jnp.float32
BF16 = jnp.bfloat16

VMEM = pltpu.VMEM
ANY = pl.ANY
SMEM = pltpu.SMEM


def nt(a, b):
    return lax.dot_general(a, b, (((1,), (1,)), ((), ())), preferred_element_type=F32)


def nn(a, b):
    return lax.dot_general(a, b, (((1,), (0,)), ((), ())), preferred_element_type=F32)


def tn(a, b):
    return lax.dot_general(a, b, (((0,), (0,)), ((), ())), preferred_element_type=F32)


def stacked(ref, g):
    return jnp.concatenate(
        [ref[:, (g * GROUP + j) * HD : (g * GROUP + j + 1) * HD] for j in range(GROUP)], axis=0
    )


def softmax_t(score):
    score = score * SCALE
    key_at = lax.broadcasted_iota(jnp.int32, (CH, GROUP * CH), 0)
    row_at = lax.broadcasted_iota(jnp.int32, (CH, GROUP * CH), 1) % CH
    own = jnp.where(key_at <= row_at, score[BLK:], -jnp.inf)
    score = jnp.concatenate([score[:BLK], own], axis=0)
    raised = jnp.exp(score - jnp.max(score, axis=0, keepdims=True))
    return raised * (1.0 / jnp.sum(raised, axis=0, keepdims=True))


def section_kernel(
    ids_h, hidb_h, hidf_h, qb_h, qf_h, g_h, pk_h, pv_h, wk_h, wv_h,
    send_h, fwd_h, back_h, pkg_h, pvg_h, gs_h, keys_h,
    ids, hid, qb, qf, g, keys, values, weight, own, fwd, back, pkg, pvg, gs, sem, wsem, osem,
):
    rows = (pl.ds(0, CH), pl.ds(CH, CH))
    prefix = pl.ds(0, BLK)
    named = pltpu.make_async_copy(ids_h, ids, sem.at[9])
    named.start()
    load = [
        pltpu.make_async_copy(hidb_h, hid.at[rows[0]], sem.at[0]),
        pltpu.make_async_copy(hidf_h, hid.at[rows[1]], sem.at[1]),
        pltpu.make_async_copy(qb_h, qb, sem.at[2]),
        pltpu.make_async_copy(g_h, g, sem.at[3]),
        pltpu.make_async_copy(qf_h, qf, sem.at[4]),
    ]
    wload = []
    for h in range(KVH):
        at = pl.ds(h * HD, HD)
        for i, src in enumerate((wk_h, wv_h)):
            to = weight.at[:, pl.ds((2 * h + i) * HD, HD)]
            wload.append(pltpu.make_async_copy(src.at[:, at], to, wsem.at[2 * h + i]))
    for copy in load[:2] + wload + load[2:]:
        copy.start()
    named.wait()
    for group, block in ((0, ids[1]), (1, ids[0])):
        for i, (src, dst) in enumerate(((pk_h, keys), (pv_h, values))):
            to = dst.at[group, prefix]
            copy = pltpu.make_async_copy(src.at[block], to, sem.at[5 + 2 * group + i])
            copy.start()
            load.append(copy)
    out = []

    def put(src, dst):
        copy = pltpu.make_async_copy(src, dst, osem.at[len(out)])
        copy.start()
        out.append(copy)

    load[0].wait()
    for t in range(CHIPS):
        put(hid.at[rows[0], pl.ds(t * ROWS, ROWS)], send_h.at[t, :, pl.ds(0, ROWS)])
    load[1].wait()

    def columns(h):
        return slice(h * HD, (h + 1) * HD)

    def project(h):
        wload[2 * h].wait()
        wload[2 * h + 1].wait()
        new = nn(hid[...], weight[:, 2 * h * HD : 2 * (h + 1) * HD]).astype(BF16)
        for group in range(2):
            keys[group, BLK:, columns(h)] = new[group * CH : (group + 1) * CH, :HD]
            values[group, BLK:, columns(h)] = new[group * CH : (group + 1) * CH, HD:]

    def backward(heads):
        query = {h: stacked(qb, h) for h in heads}
        grad = {h: stacked(g, h) for h in heads}
        score = {h: nt(keys[0, :, columns(h)], query[h]) for h in heads}
        grad_probs = {h: nt(values[0, :, columns(h)], grad[h]) for h in heads}
        for h in heads:
            probs = softmax_t(score[h])
            inner = jnp.sum(probs * grad_probs[h], axis=0, keepdims=True)
            grad_scores = (probs * (grad_probs[h] - inner) * SCALE).astype(BF16)
            gs[h] = grad_scores
            key_grads = nn(grad_scores, query[h])
            value_grads = nn(probs.astype(BF16), grad[h])
            own[:, 2 * h * HD : (2 * h + 1) * HD] = key_grads[BLK:].astype(BF16)
            own[:, (2 * h + 1) * HD : 2 * (h + 1) * HD] = value_grads[BLK:].astype(BF16)
            pkg[:, columns(h)] = key_grads[:BLK].astype(BF16)
            pvg[:, columns(h)] = value_grads[:BLK].astype(BF16)

    def forward(heads):
        score = {h: nt(keys[1, :, columns(h)], stacked(qf, h)) for h in heads}
        for h in heads:
            attended = tn(softmax_t(score[h]).astype(BF16), values[1, :, columns(h)])
            for j in range(GROUP):
                at = columns(h * GROUP + j)
                fwd[:, at] = (
                    hid[CH:, at].astype(F32) + attended[j * CH : (j + 1) * CH]
                ).astype(BF16)

    def backed():
        for c in range(CHUNKS):
            at = slice(c * STEP, (c + 1) * STEP)
            back[:, at] = (g[:, at].astype(F32) + nt(own[...], weight[at, :])).astype(BF16)

    def sent():
        for t in range(CHIPS):
            put(own, send_h.at[t, :, pl.ds(ROWS, 2 * KVW)])
        put(pkg, pkg_h)
        put(pvg, pvg_h)
        put(gs, gs_h)
        put(keys.at[0], keys_h)

    for h in range(KVH):
        project(h)
    for copy in load[2:]:
        copy.wait()
    backward(range(KVH))
    sent()
    forward(range(KVH))
    backed()
    put(back, back_h)
    put(fwd, fwd_h)
    for copy in out:
        copy.wait()


def query_kernel(gs, keys, out):
    for h in range(KVH):
        grad = tn(gs[h], keys[:, h * HD : (h + 1) * HD])
        for j in range(GROUP):
            cols = slice((h * GROUP + j) * HD, (h * GROUP + j + 1) * HD)
            out[:, cols] = grad[j * CH : (j + 1) * CH].astype(BF16)


def weight_kernel(core, recv, mine, theirs):
    here = core[0]
    grads = recv[:, :, ROWS:].reshape(CHIPS * CH, 2 * KVW)
    low = tn(recv[:, :, :HALF].reshape(CHIPS * CH, HALF), grads)
    high = tn(recv[:, :, HALF:ROWS].reshape(CHIPS * CH, HALF), grads)
    first = here == 0
    mine[...] = jnp.where(first, low, high)
    theirs[...] = jnp.where(first, high, low).astype(BF16)


def sum_kernel(core, mine, both, fwd_in, back_in, key_grad, value_grad, fwd_out, back_out, sem):
    moves = [
        pltpu.make_async_copy(fwd_in, fwd_out, sem.at[0]),
        pltpu.make_async_copy(back_in, back_out, sem.at[1]),
    ]
    for copy in moves:
        copy.start()
    total = mine[...] + both[1 - core[0]].astype(F32)
    for h in range(KVH):
        at = slice(h * HD, (h + 1) * HD)
        key_grad[:, at] = total[:, 2 * h * HD : (2 * h + 1) * HD].astype(BF16)
        value_grad[:, at] = total[:, (2 * h + 1) * HD : 2 * (h + 1) * HD].astype(BF16)
    for copy in moves:
        copy.wait()


def call(kernel, outs, scratch, flops, in_specs, out_specs, size=62):
    return pl.pallas_call(
        kernel,
        out_shape=[jax.ShapeDtypeStruct(s, t) for s, t in outs],
        in_specs=in_specs,
        out_specs=out_specs,
        scratch_shapes=scratch,
        compiler_params=pltpu.CompilerParams(vmem_limit_bytes=size * 1024 * 1024),
        cost_estimate=pl.CostEstimate(flops=flops, bytes_accessed=6 << 20, transcendentals=200000),
    )


def spec(space):
    return pl.BlockSpec(memory_space=space)


def section_call(*arrays):
    dma = pltpu.SemaphoreType.DMA
    wide, kv = (CH, D), (KEYS, KVW)
    return call(
        section_kernel,
        [
            ((CHIPS, CH, ROWS + 2 * KVW), BF16),
            (wide, BF16),
            (wide, BF16),
            ((BLK, KVW), BF16),
            ((BLK, KVW), BF16),
            ((KVH, KEYS, GROUP * CH), BF16),
            (kv, BF16),
        ],
        [SMEM((2,), jnp.int32), VMEM((2 * CH, D), BF16)]
        + [VMEM(wide, BF16)] * 3
        + [VMEM((2,) + kv, BF16)] * 2
        + [VMEM((D, 2 * KVW), BF16), VMEM((CH, 2 * KVW), BF16)]
        + [VMEM(wide, BF16)] * 2
        + [VMEM((BLK, KVW), BF16)] * 2
        + [VMEM((KVH, KEYS, GROUP * CH), BF16), dma((10,)), dma((2 * KVH,)), dma((22,))],
        1_600_000_000,
        [spec(ANY)] * 10,
        [spec(ANY)] * 7,
    )(*arrays)


def along(value, axis, steps, wrap):
    count = lax.axis_size(axis)
    pairs = [(i, (i + steps) % count) for i in range(count) if wrap or 0 <= i + steps < count]
    return lax.ppermute(value, axis, pairs)


def per_device(
    fwd_hidden, fwd_query, bwd_hidden, bwd_query, bwd_grad,
    prefix_keys, prefix_values, key_weight, value_weight, block_ids,
):
    count = lax.axis_size("dp")
    dma = pltpu.SemaphoreType.DMA
    wide = (CH, D)
    ids = block_ids.reshape(2)
    send, out_fwd, out_bwd, pkg, pvg, gs, keys_bwd = section_call(
        ids, bwd_hidden[0, 0], fwd_hidden[0, 0], bwd_query[0, 0], fwd_query[0, 0], bwd_grad[0, 0],
        prefix_keys[0, 0], prefix_values[0, 0], key_weight[0], value_weight[0],
    )
    same_core = [[2 * t + c for t in range(count // 2)] for c in range(2)]
    pairs = [[2 * t, 2 * t + 1] for t in range(count // 2)]
    recv = lax.all_to_all(send, "dp", 0, 0, tiled=True, axis_index_groups=same_core)
    next_hidden = along(out_fwd, "section", 1, True)
    prev_grad = along(out_bwd, "section", -1, False)
    (query_grad,) = call(
        query_kernel,
        [(wide, BF16)],
        [],
        100_000_000,
        [spec(VMEM)] * 2,
        [spec(VMEM)],
        16,
    )(gs, keys_bwd)
    core = lax.axis_index("dp") & 1
    mine, theirs = call(
        weight_kernel,
        [((HALF, 2 * KVW), F32), ((HALF, 2 * KVW), BF16)],
        [],
        270_000_000,
        [spec(SMEM), spec(VMEM)],
        [spec(VMEM)] * 2,
        16,
    )(core.reshape(1), recv)
    both = lax.all_gather(theirs, "dp", axis=0, axis_index_groups=pairs)
    key_weight_grad, value_weight_grad, next_hidden, prev_grad = call(
        sum_kernel,
        [((HALF, KVW), BF16)] * 2 + [(wide, BF16)] * 2,
        [dma((2,))],
        1_000_000,
        [spec(SMEM)] + [spec(VMEM)] * 2 + [spec(ANY)] * 2,
        [spec(VMEM)] * 2 + [spec(ANY)] * 2,
        16,
    )(core.reshape(1), mine, both, next_hidden, prev_grad)
    return (
        next_hidden[None, None],
        prev_grad[None, None],
        query_grad[None, None],
        pkg[None, None, None],
        pvg[None, None, None],
        key_weight_grad[None],
        value_weight_grad[None],
    )


def solution(mesh):
    device = P("section", "dp")
    return jax.shard_map(
        per_device,
        mesh=mesh,
        in_specs=(device,) * 7 + (P("section"),) * 2 + (device,),
        out_specs=(device,) * 5 + (P("section", "dp"),) * 2,
        check_vma=False,
    )
```

```python
import functools

import jax
import jax.numpy as jnp
from jax import lax
from jax.experimental import pallas as pl
from jax.experimental.pallas import tpu as pltpu
from jax.sharding import PartitionSpec as P

HEADS = 16
KVH = 4
HD = 128
GROUP = HEADS // KVH
D = 2048
CH = 64
BLK = 128
KVW = KVH * HD
KEYS = BLK + CH
SCALE = HD ** (-0.5)
CHIPS = 8
ROWS = D // CHIPS
HALF = ROWS // 2
CHUNKS = 4
STEP = D // CHUNKS
F32 = jnp.float32
BF16 = jnp.bfloat16

VMEM = pltpu.VMEM
ANY = pl.ANY
SMEM = pltpu.SMEM


def nt(a, b):
    return lax.dot_general(a, b, (((1,), (1,)), ((), ())), preferred_element_type=F32)


def nn(a, b):
    return lax.dot_general(a, b, (((1,), (0,)), ((), ())), preferred_element_type=F32)


def tn(a, b):
    return lax.dot_general(a, b, (((0,), (0,)), ((), ())), preferred_element_type=F32)


def stacked(ref, g):
    return jnp.concatenate(
        [ref[:, (g * GROUP + j) * HD : (g * GROUP + j + 1) * HD] for j in range(GROUP)], axis=0
    )


def softmax_t(score):
    score = score * SCALE
    key_at = lax.broadcasted_iota(jnp.int32, (CH, GROUP * CH), 0)
    row_at = lax.broadcasted_iota(jnp.int32, (CH, GROUP * CH), 1) % CH
    own = jnp.where(key_at <= row_at, score[BLK:], -jnp.inf)
    score = jnp.concatenate([score[:BLK], own], axis=0)
    raised = jnp.exp(score - jnp.max(score, axis=0, keepdims=True))
    return raised * (1.0 / jnp.sum(raised, axis=0, keepdims=True))


def section_kernel(
    ids_h, hidb_h, hidf_h, qb_h, qf_h, g_h, pk_h, pv_h, wk_h, wv_h,
    send_h, fwd_h, back_h, pkg_h, pvg_h, gs_h, keys_h,
    ids, hid, qb, qf, g, keys, values, weight, own, fwd, back, pkg, pvg, gs, sem, wsem, osem,
):
    rows = (pl.ds(0, CH), pl.ds(CH, CH))
    prefix = pl.ds(0, BLK)
    named = pltpu.make_async_copy(ids_h, ids, sem.at[9])
    named.start()
    load = [
        pltpu.make_async_copy(hidb_h, hid.at[rows[0]], sem.at[0]),
        pltpu.make_async_copy(hidf_h, hid.at[rows[1]], sem.at[1]),
        pltpu.make_async_copy(qb_h, qb, sem.at[2]),
        pltpu.make_async_copy(g_h, g, sem.at[3]),
        pltpu.make_async_copy(qf_h, qf, sem.at[4]),
    ]
    wload = []
    for h in range(KVH):
        at = pl.ds(h * HD, HD)
        for i, src in enumerate((wk_h, wv_h)):
            to = weight.at[:, pl.ds((2 * h + i) * HD, HD)]
            wload.append(pltpu.make_async_copy(src.at[:, at], to, wsem.at[2 * h + i]))
    for copy in load[:2] + wload + load[2:]:
        copy.start()
    named.wait()
    for group, block in ((0, ids[1]), (1, ids[0])):
        for i, (src, dst) in enumerate(((pk_h, keys), (pv_h, values))):
            to = dst.at[group, prefix]
            copy = pltpu.make_async_copy(src.at[block], to, sem.at[5 + 2 * group + i])
            copy.start()
            load.append(copy)
    out = []

    def put(src, dst):
        copy = pltpu.make_async_copy(src, dst, osem.at[len(out)])
        copy.start()
        out.append(copy)

    load[0].wait()
    for t in range(CHIPS):
        put(hid.at[rows[0], pl.ds(t * ROWS, ROWS)], send_h.at[t, :, pl.ds(0, ROWS)])
    load[1].wait()

    def columns(h):
        return slice(h * HD, (h + 1) * HD)

    def project(h):
        wload[2 * h].wait()
        wload[2 * h + 1].wait()
        new = nn(hid[...], weight[:, 2 * h * HD : 2 * (h + 1) * HD]).astype(BF16)
        for group in range(2):
            keys[group, BLK:, columns(h)] = new[group * CH : (group + 1) * CH, :HD]
            values[group, BLK:, columns(h)] = new[group * CH : (group + 1) * CH, HD:]

    def backward(heads):
        query = {h: stacked(qb, h) for h in heads}
        grad = {h: stacked(g, h) for h in heads}
        score = {h: nt(keys[0, :, columns(h)], query[h]) for h in heads}
        grad_probs = {h: nt(values[0, :, columns(h)], grad[h]) for h in heads}
        for h in heads:
            probs = softmax_t(score[h])
            inner = jnp.sum(probs * grad_probs[h], axis=0, keepdims=True)
            grad_scores = (probs * (grad_probs[h] - inner) * SCALE).astype(BF16)
            gs[h] = grad_scores
            key_grads = nn(grad_scores, query[h])
            value_grads = nn(probs.astype(BF16), grad[h])
            own[:, 2 * h * HD : (2 * h + 1) * HD] = key_grads[BLK:].astype(BF16)
            own[:, (2 * h + 1) * HD : 2 * (h + 1) * HD] = value_grads[BLK:].astype(BF16)
            pkg[:, columns(h)] = key_grads[:BLK].astype(BF16)
            pvg[:, columns(h)] = value_grads[:BLK].astype(BF16)

    def forward(heads):
        score = {h: nt(keys[1, :, columns(h)], stacked(qf, h)) for h in heads}
        for h in heads:
            attended = tn(softmax_t(score[h]).astype(BF16), values[1, :, columns(h)])
            for j in range(GROUP):
                at = columns(h * GROUP + j)
                fwd[:, at] = (
                    hid[CH:, at].astype(F32) + attended[j * CH : (j + 1) * CH]
                ).astype(BF16)

    def backed():
        for c in range(CHUNKS):
            at = slice(c * STEP, (c + 1) * STEP)
            back[:, at] = (g[:, at].astype(F32) + nt(own[...], weight[at, :])).astype(BF16)

    def sent():
        for t in range(CHIPS):
            put(own, send_h.at[t, :, pl.ds(ROWS, 2 * KVW)])
        put(pkg, pkg_h)
        put(pvg, pvg_h)
        put(gs, gs_h)
        put(keys.at[0], keys_h)

    for h in range(KVH):
        project(h)
    for copy in load[2:]:
        copy.wait()
    backward(range(KVH))
    sent()
    forward(range(KVH))
    backed()
    put(back, back_h)
    put(fwd, fwd_h)
    for copy in out:
        copy.wait()


def query_kernel(gs, keys, out):
    for h in range(KVH):
        grad = tn(gs[h], keys[:, h * HD : (h + 1) * HD])
        for j in range(GROUP):
            cols = slice((h * GROUP + j) * HD, (h * GROUP + j + 1) * HD)
            out[:, cols] = grad[j * CH : (j + 1) * CH].astype(BF16)


def weight_kernel(core, recv, mine, theirs):
    here = core[0]
    grads = recv[:, :, ROWS:].reshape(CHIPS * CH, 2 * KVW)
    low = tn(recv[:, :, :HALF].reshape(CHIPS * CH, HALF), grads)
    high = tn(recv[:, :, HALF:ROWS].reshape(CHIPS * CH, HALF), grads)
    first = here == 0
    mine[...] = jnp.where(first, low, high)
    theirs[...] = jnp.where(first, high, low).astype(BF16)


def sum_kernel(
    core, mine, both, fwd_in, back_in,
    key_out, value_out, fwd_out, back_out,
    key_grad, value_grad, sem,
):
    moves = [
        pltpu.make_async_copy(fwd_in, fwd_out, sem.at[0]),
        pltpu.make_async_copy(back_in, back_out, sem.at[1]),
        pltpu.make_async_copy(key_grad, key_out, sem.at[2]),
        pltpu.make_async_copy(value_grad, value_out, sem.at[3]),
    ]
    for copy in moves[:2]:
        copy.start()
    total = mine[...] + both[1 - core[0]].astype(F32)
    for h in range(KVH):
        at = slice(h * HD, (h + 1) * HD)
        key_grad[:, at] = total[:, 2 * h * HD : (2 * h + 1) * HD].astype(BF16)
        value_grad[:, at] = total[:, (2 * h + 1) * HD : 2 * (h + 1) * HD].astype(BF16)
    for copy in moves[2:]:
        copy.start()
    for copy in moves:
        copy.wait()


def call(kernel, outs, scratch, flops, in_specs, out_specs, size=62):
    return pl.pallas_call(
        kernel,
        out_shape=[jax.ShapeDtypeStruct(s, t) for s, t in outs],
        in_specs=in_specs,
        out_specs=out_specs,
        scratch_shapes=scratch,
        compiler_params=pltpu.CompilerParams(vmem_limit_bytes=size * 1024 * 1024),
        cost_estimate=pl.CostEstimate(flops=flops, bytes_accessed=6 << 20, transcendentals=200000),
    )


def spec(space):
    return pl.BlockSpec(memory_space=space)


def section_call(*arrays):
    dma = pltpu.SemaphoreType.DMA
    wide, kv = (CH, D), (KEYS, KVW)
    return call(
        section_kernel,
        [
            ((CHIPS, CH, ROWS + 2 * KVW), BF16),
            (wide, BF16),
            (wide, BF16),
            ((BLK, KVW), BF16),
            ((BLK, KVW), BF16),
            ((KVH, KEYS, GROUP * CH), BF16),
            (kv, BF16),
        ],
        [SMEM((2,), jnp.int32), VMEM((2 * CH, D), BF16)]
        + [VMEM(wide, BF16)] * 3
        + [VMEM((2,) + kv, BF16)] * 2
        + [VMEM((D, 2 * KVW), BF16), VMEM((CH, 2 * KVW), BF16)]
        + [VMEM(wide, BF16)] * 2
        + [VMEM((BLK, KVW), BF16)] * 2
        + [VMEM((KVH, KEYS, GROUP * CH), BF16), dma((10,)), dma((2 * KVH,)), dma((22,))],
        1_600_000_000,
        [spec(ANY)] * 10,
        [spec(ANY)] * 7,
    )(*arrays)


def along(value, axis, steps, wrap):
    count = lax.axis_size(axis)
    pairs = [(i, (i + steps) % count) for i in range(count) if wrap or 0 <= i + steps < count]
    return lax.ppermute(value, axis, pairs)


def per_device(
    fwd_hidden, fwd_query, bwd_hidden, bwd_query, bwd_grad,
    prefix_keys, prefix_values, key_weight, value_weight, block_ids,
):
    count = lax.axis_size("dp")
    dma = pltpu.SemaphoreType.DMA
    wide = (CH, D)
    ids = block_ids.reshape(2)
    send, out_fwd, out_bwd, pkg, pvg, gs, keys_bwd = section_call(
        ids, bwd_hidden[0, 0], fwd_hidden[0, 0], bwd_query[0, 0], fwd_query[0, 0], bwd_grad[0, 0],
        prefix_keys[0, 0], prefix_values[0, 0], key_weight[0], value_weight[0],
    )
    same_core = [[2 * t + c for t in range(count // 2)] for c in range(2)]
    pairs = [[2 * t, 2 * t + 1] for t in range(count // 2)]
    recv = lax.all_to_all(send, "dp", 0, 0, tiled=True, axis_index_groups=same_core)
    next_hidden = along(out_fwd, "section", 1, True)
    prev_grad = along(out_bwd, "section", -1, False)
    (query_grad,) = call(
        query_kernel,
        [(wide, BF16)],
        [],
        100_000_000,
        [spec(VMEM)] * 2,
        [spec(VMEM)],
        16,
    )(gs, keys_bwd)
    core = lax.axis_index("dp") & 1
    mine, theirs = call(
        weight_kernel,
        [((HALF, 2 * KVW), F32), ((HALF, 2 * KVW), BF16)],
        [],
        270_000_000,
        [spec(SMEM), spec(VMEM)],
        [spec(VMEM)] * 2,
        16,
    )(core.reshape(1), recv)
    both = lax.all_gather(theirs, "dp", axis=0, axis_index_groups=pairs)
    key_weight_grad, value_weight_grad, next_hidden, prev_grad = call(
        sum_kernel,
        [((HALF, KVW), BF16)] * 2 + [(wide, BF16)] * 2,
        [VMEM((HALF, KVW), BF16)] * 2 + [dma((4,))],
        1_000_000,
        [spec(SMEM)] + [spec(VMEM)] * 2 + [spec(ANY)] * 2,
        [spec(ANY)] * 4,
        16,
    )(core.reshape(1), mine, both, next_hidden, prev_grad)
    return (
        next_hidden[None, None],
        prev_grad[None, None],
        query_grad[None, None],
        pkg[None, None, None],
        pvg[None, None, None],
        key_weight_grad[None],
        value_weight_grad[None],
    )


def solution(mesh):
    device = P("section", "dp")
    return jax.shard_map(
        per_device,
        mesh=mesh,
        in_specs=(device,) * 7 + (P("section"),) * 2 + (device,),
        out_specs=(device,) * 5 + (P("section", "dp"),) * 2,
        check_vma=False,
    )
```

```python
import functools

import jax
import jax.numpy as jnp
from jax import lax
from jax.experimental import pallas as pl
from jax.experimental.pallas import tpu as pltpu
from jax.sharding import PartitionSpec as P

HEADS = 16
KVH = 4
HD = 128
GROUP = HEADS // KVH
D = 2048
CH = 64
BLK = 128
KVW = KVH * HD
KEYS = BLK + CH
SCALE = HD ** (-0.5)
CHIPS = 8
ROWS = D // CHIPS
HALF = ROWS // 2
CHUNKS = 4
STEP = D // CHUNKS
F32 = jnp.float32
BF16 = jnp.bfloat16

VMEM = pltpu.VMEM
ANY = pl.ANY
SMEM = pltpu.SMEM


def nt(a, b):
    return lax.dot_general(a, b, (((1,), (1,)), ((), ())), preferred_element_type=F32)


def nn(a, b):
    return lax.dot_general(a, b, (((1,), (0,)), ((), ())), preferred_element_type=F32)


def tn(a, b):
    return lax.dot_general(a, b, (((0,), (0,)), ((), ())), preferred_element_type=F32)


def stacked(ref, g):
    return jnp.concatenate(
        [ref[:, (g * GROUP + j) * HD : (g * GROUP + j + 1) * HD] for j in range(GROUP)], axis=0
    )


def softmax_t(score):
    score = score * SCALE
    key_at = lax.broadcasted_iota(jnp.int32, (CH, GROUP * CH), 0)
    row_at = lax.broadcasted_iota(jnp.int32, (CH, GROUP * CH), 1) % CH
    own = jnp.where(key_at <= row_at, score[BLK:], -jnp.inf)
    score = jnp.concatenate([score[:BLK], own], axis=0)
    raised = jnp.exp(score - jnp.max(score, axis=0, keepdims=True))
    return raised * (1.0 / jnp.sum(raised, axis=0, keepdims=True))


def section_kernel(
    ids_h, hidb_h, hidf_h, qb_h, qf_h, g_h, pk_h, pv_h, wk_h, wv_h,
    send_h, fwd_h, back_h, pkg_h, pvg_h, gs_h, keys_h,
    ids, hid, qb, qf, g, keys, values, weight, own, fwd, back, pkg, pvg, gs, sem, wsem, osem,
):
    rows = (pl.ds(0, CH), pl.ds(CH, CH))
    prefix = pl.ds(0, BLK)
    named = pltpu.make_async_copy(ids_h, ids, sem.at[9])
    named.start()
    load = [
        pltpu.make_async_copy(hidb_h, hid.at[rows[0]], sem.at[0]),
        pltpu.make_async_copy(hidf_h, hid.at[rows[1]], sem.at[1]),
        pltpu.make_async_copy(qb_h, qb, sem.at[2]),
        pltpu.make_async_copy(g_h, g, sem.at[3]),
        pltpu.make_async_copy(qf_h, qf, sem.at[4]),
    ]
    wload = []
    for c in range(CHUNKS):
        at = pl.ds(c * STEP, STEP)
        for i, src in enumerate((wk_h, wv_h)):
            to = weight.at[at, pl.ds(i * KVW, KVW)]
            wload.append(pltpu.make_async_copy(src.at[at], to, wsem.at[2 * c + i]))
    for copy in load[:2] + wload + load[2:]:
        copy.start()
    named.wait()
    for group, block in ((0, ids[1]), (1, ids[0])):
        for i, (src, dst) in enumerate(((pk_h, keys), (pv_h, values))):
            to = dst.at[group, prefix]
            copy = pltpu.make_async_copy(src.at[block], to, sem.at[5 + 2 * group + i])
            copy.start()
            load.append(copy)
    out = []

    def put(src, dst):
        copy = pltpu.make_async_copy(src, dst, osem.at[len(out)])
        copy.start()
        out.append(copy)

    load[0].wait()
    for t in range(CHIPS):
        put(hid.at[rows[0], pl.ds(t * ROWS, ROWS)], send_h.at[t, :, pl.ds(0, ROWS)])
    load[1].wait()

    def columns(h):
        return slice(h * HD, (h + 1) * HD)

    def project():
        total = None
        for c in range(CHUNKS):
            wload[2 * c].wait()
            wload[2 * c + 1].wait()
            at = slice(c * STEP, (c + 1) * STEP)
            part = nn(hid[:, at], weight[at, :])
            total = part if total is None else total + part
        new = total.astype(BF16)
        for group in range(2):
            keys[group, BLK:, :] = new[group * CH : (group + 1) * CH, :KVW]
            values[group, BLK:, :] = new[group * CH : (group + 1) * CH, KVW:]

    def backward(heads):
        query = {h: stacked(qb, h) for h in heads}
        grad = {h: stacked(g, h) for h in heads}
        score = {h: nt(keys[0, :, columns(h)], query[h]) for h in heads}
        grad_probs = {h: nt(values[0, :, columns(h)], grad[h]) for h in heads}
        for h in heads:
            probs = softmax_t(score[h])
            inner = jnp.sum(probs * grad_probs[h], axis=0, keepdims=True)
            grad_scores = (probs * (grad_probs[h] - inner) * SCALE).astype(BF16)
            gs[h] = grad_scores
            key_grads = nn(grad_scores, query[h])
            value_grads = nn(probs.astype(BF16), grad[h])
            own[:, columns(h)] = key_grads[BLK:].astype(BF16)
            own[:, columns(KVH + h)] = value_grads[BLK:].astype(BF16)
            pkg[:, columns(h)] = key_grads[:BLK].astype(BF16)
            pvg[:, columns(h)] = value_grads[:BLK].astype(BF16)

    def forward(heads):
        score = {h: nt(keys[1, :, columns(h)], stacked(qf, h)) for h in heads}
        for h in heads:
            attended = tn(softmax_t(score[h]).astype(BF16), values[1, :, columns(h)])
            for j in range(GROUP):
                at = columns(h * GROUP + j)
                fwd[:, at] = (
                    hid[CH:, at].astype(F32) + attended[j * CH : (j + 1) * CH]
                ).astype(BF16)

    def backed():
        for c in range(CHUNKS):
            at = slice(c * STEP, (c + 1) * STEP)
            back[:, at] = (g[:, at].astype(F32) + nt(own[...], weight[at, :])).astype(BF16)

    def sent():
        for t in range(CHIPS):
            put(own, send_h.at[t, :, pl.ds(ROWS, 2 * KVW)])
        put(pkg, pkg_h)
        put(pvg, pvg_h)
        put(gs, gs_h)
        put(keys.at[0], keys_h)

    project()
    for copy in load[2:]:
        copy.wait()
    backward(range(KVH))
    sent()
    forward(range(KVH))
    backed()
    put(back, back_h)
    put(fwd, fwd_h)
    for copy in out:
        copy.wait()


def query_kernel(gs, keys, out):
    for h in range(KVH):
        grad = tn(gs[h], keys[:, h * HD : (h + 1) * HD])
        for j in range(GROUP):
            cols = slice((h * GROUP + j) * HD, (h * GROUP + j + 1) * HD)
            out[:, cols] = grad[j * CH : (j + 1) * CH].astype(BF16)


def weight_kernel(core, recv, mine, theirs):
    here = core[0]
    grads = recv[:, :, ROWS:].reshape(CHIPS * CH, 2 * KVW)
    low = tn(recv[:, :, :HALF].reshape(CHIPS * CH, HALF), grads)
    high = tn(recv[:, :, HALF:ROWS].reshape(CHIPS * CH, HALF), grads)
    first = here == 0
    mine[...] = jnp.where(first, low, high)
    theirs[...] = jnp.where(first, high, low).astype(BF16)


def sum_kernel(
    core, mine, both, fwd_in, back_in,
    key_out, value_out, fwd_out, back_out,
    key_grad, value_grad, sem,
):
    moves = [
        pltpu.make_async_copy(fwd_in, fwd_out, sem.at[0]),
        pltpu.make_async_copy(back_in, back_out, sem.at[1]),
        pltpu.make_async_copy(key_grad, key_out, sem.at[2]),
        pltpu.make_async_copy(value_grad, value_out, sem.at[3]),
    ]
    for copy in moves[:2]:
        copy.start()
    total = mine[...] + both[1 - core[0]].astype(F32)
    key_grad[...] = total[:, :KVW].astype(BF16)
    value_grad[...] = total[:, KVW:].astype(BF16)
    for copy in moves[2:]:
        copy.start()
    for copy in moves:
        copy.wait()


def call(kernel, outs, scratch, flops, in_specs, out_specs, size=62):
    return pl.pallas_call(
        kernel,
        out_shape=[jax.ShapeDtypeStruct(s, t) for s, t in outs],
        in_specs=in_specs,
        out_specs=out_specs,
        scratch_shapes=scratch,
        compiler_params=pltpu.CompilerParams(vmem_limit_bytes=size * 1024 * 1024),
        cost_estimate=pl.CostEstimate(flops=flops, bytes_accessed=6 << 20, transcendentals=200000),
    )


def spec(space):
    return pl.BlockSpec(memory_space=space)


def section_call(*arrays):
    dma = pltpu.SemaphoreType.DMA
    wide, kv = (CH, D), (KEYS, KVW)
    return call(
        section_kernel,
        [
            ((CHIPS, CH, ROWS + 2 * KVW), BF16),
            (wide, BF16),
            (wide, BF16),
            ((BLK, KVW), BF16),
            ((BLK, KVW), BF16),
            ((KVH, KEYS, GROUP * CH), BF16),
            (kv, BF16),
        ],
        [SMEM((2,), jnp.int32), VMEM((2 * CH, D), BF16)]
        + [VMEM(wide, BF16)] * 3
        + [VMEM((2,) + kv, BF16)] * 2
        + [VMEM((D, 2 * KVW), BF16), VMEM((CH, 2 * KVW), BF16)]
        + [VMEM(wide, BF16)] * 2
        + [VMEM((BLK, KVW), BF16)] * 2
        + [VMEM((KVH, KEYS, GROUP * CH), BF16), dma((10,)), dma((2 * CHUNKS,)), dma((22,))],
        1_600_000_000,
        [spec(ANY)] * 10,
        [spec(ANY)] * 7,
    )(*arrays)


def along(value, axis, steps, wrap):
    count = lax.axis_size(axis)
    pairs = [(i, (i + steps) % count) for i in range(count) if wrap or 0 <= i + steps < count]
    return lax.ppermute(value, axis, pairs)


def per_device(
    fwd_hidden, fwd_query, bwd_hidden, bwd_query, bwd_grad,
    prefix_keys, prefix_values, key_weight, value_weight, block_ids,
):
    count = lax.axis_size("dp")
    dma = pltpu.SemaphoreType.DMA
    wide = (CH, D)
    ids = block_ids.reshape(2)
    send, out_fwd, out_bwd, pkg, pvg, gs, keys_bwd = section_call(
        ids, bwd_hidden[0, 0], fwd_hidden[0, 0], bwd_query[0, 0], fwd_query[0, 0], bwd_grad[0, 0],
        prefix_keys[0, 0], prefix_values[0, 0], key_weight[0], value_weight[0],
    )
    same_core = [[2 * t + c for t in range(count // 2)] for c in range(2)]
    pairs = [[2 * t, 2 * t + 1] for t in range(count // 2)]
    recv = lax.all_to_all(send, "dp", 0, 0, tiled=True, axis_index_groups=same_core)
    next_hidden = along(out_fwd, "section", 1, True)
    prev_grad = along(out_bwd, "section", -1, False)
    (query_grad,) = call(
        query_kernel,
        [(wide, BF16)],
        [],
        100_000_000,
        [spec(VMEM)] * 2,
        [spec(VMEM)],
        16,
    )(gs, keys_bwd)
    core = lax.axis_index("dp") & 1
    mine, theirs = call(
        weight_kernel,
        [((HALF, 2 * KVW), F32), ((HALF, 2 * KVW), BF16)],
        [],
        270_000_000,
        [spec(SMEM), spec(VMEM)],
        [spec(VMEM)] * 2,
        16,
    )(core.reshape(1), recv)
    both = lax.all_gather(theirs, "dp", axis=0, axis_index_groups=pairs)
    key_weight_grad, value_weight_grad, next_hidden, prev_grad = call(
        sum_kernel,
        [((HALF, KVW), BF16)] * 2 + [(wide, BF16)] * 2,
        [VMEM((HALF, KVW), BF16)] * 2 + [dma((4,))],
        1_000_000,
        [spec(SMEM)] + [spec(VMEM)] * 2 + [spec(ANY)] * 2,
        [spec(ANY)] * 4,
        16,
    )(core.reshape(1), mine, both, next_hidden, prev_grad)
    return (
        next_hidden[None, None],
        prev_grad[None, None],
        query_grad[None, None],
        pkg[None, None, None],
        pvg[None, None, None],
        key_weight_grad[None],
        value_weight_grad[None],
    )


def solution(mesh):
    device = P("section", "dp")
    return jax.shard_map(
        per_device,
        mesh=mesh,
        in_specs=(device,) * 7 + (P("section"),) * 2 + (device,),
        out_specs=(device,) * 5 + (P("section", "dp"),) * 2,
        check_vma=False,
    )
```

```python
import functools

import jax
import jax.numpy as jnp
from jax import lax
from jax.experimental import pallas as pl
from jax.experimental.pallas import tpu as pltpu
from jax.sharding import PartitionSpec as P

HEADS = 16
KVH = 4
HD = 128
GROUP = HEADS // KVH
D = 2048
CH = 64
BLK = 128
KVW = KVH * HD
KEYS = BLK + CH
SCALE = HD ** (-0.5)
CHIPS = 8
ROWS = D // CHIPS
HALF = ROWS // 2
CHUNKS = 4
STEP = D // CHUNKS
F32 = jnp.float32
BF16 = jnp.bfloat16

VMEM = pltpu.VMEM
ANY = pl.ANY
SMEM = pltpu.SMEM


def nt(a, b):
    return lax.dot_general(a, b, (((1,), (1,)), ((), ())), preferred_element_type=F32)


def nn(a, b):
    return lax.dot_general(a, b, (((1,), (0,)), ((), ())), preferred_element_type=F32)


def tn(a, b):
    return lax.dot_general(a, b, (((0,), (0,)), ((), ())), preferred_element_type=F32)


def stacked(ref, g):
    return jnp.concatenate(
        [ref[:, (g * GROUP + j) * HD : (g * GROUP + j + 1) * HD] for j in range(GROUP)], axis=0
    )


def softmax_t(score):
    score = score * SCALE
    key_at = lax.broadcasted_iota(jnp.int32, (CH, GROUP * CH), 0)
    row_at = lax.broadcasted_iota(jnp.int32, (CH, GROUP * CH), 1) % CH
    own = jnp.where(key_at <= row_at, score[BLK:], -jnp.inf)
    score = jnp.concatenate([score[:BLK], own], axis=0)
    raised = jnp.exp(score - jnp.max(score, axis=0, keepdims=True))
    return raised * (1.0 / jnp.sum(raised, axis=0, keepdims=True))


def section_kernel(
    ids_h, hidb_h, hidf_h, qb_h, qf_h, g_h, pk_h, pv_h, wk_h, wv_h,
    send_h, fwd_h, back_h, pkg_h, pvg_h, gs_h, keys_h,
    ids, hid, qb, qf, g, keys, values, weight, own, fwd, back, pkg, pvg, gs, sem, wsem, osem,
):
    rows = (pl.ds(0, CH), pl.ds(CH, CH))
    prefix = pl.ds(0, BLK)
    named = pltpu.make_async_copy(ids_h, ids, sem.at[9])
    named.start()
    load = [
        pltpu.make_async_copy(hidb_h, hid.at[rows[0]], sem.at[0]),
        pltpu.make_async_copy(hidf_h, hid.at[rows[1]], sem.at[1]),
        pltpu.make_async_copy(qb_h, qb, sem.at[2]),
        pltpu.make_async_copy(g_h, g, sem.at[3]),
        pltpu.make_async_copy(qf_h, qf, sem.at[4]),
    ]
    wload = []
    for c in range(CHUNKS):
        at = pl.ds(c * STEP, STEP)
        for i, src in enumerate((wk_h, wv_h)):
            to = weight.at[at, pl.ds(i * KVW, KVW)]
            wload.append(pltpu.make_async_copy(src.at[at], to, wsem.at[2 * c + i]))
    for copy in load[:2] + wload + load[2:]:
        copy.start()
    named.wait()
    for group, block in ((0, ids[1]), (1, ids[0])):
        for i, (src, dst) in enumerate(((pk_h, keys), (pv_h, values))):
            to = dst.at[group, prefix]
            copy = pltpu.make_async_copy(src.at[block], to, sem.at[5 + 2 * group + i])
            copy.start()
            load.append(copy)
    out = []

    def put(src, dst):
        copy = pltpu.make_async_copy(src, dst, osem.at[len(out)])
        copy.start()
        out.append(copy)

    load[0].wait()
    for t in range(CHIPS):
        put(hid.at[rows[0], pl.ds(t * ROWS, ROWS)], send_h.at[t, :, pl.ds(0, ROWS)])
    load[1].wait()

    def columns(h):
        return slice(h * HD, (h + 1) * HD)

    def project():
        total = None
        for c in range(CHUNKS):
            wload[2 * c].wait()
            wload[2 * c + 1].wait()
            at = slice(c * STEP, (c + 1) * STEP)
            part = nn(hid[:, at], weight[at, :])
            total = part if total is None else total + part
        new = total.astype(BF16)
        for group in range(2):
            keys[group, BLK:, :] = new[group * CH : (group + 1) * CH, :KVW]
            values[group, BLK:, :] = new[group * CH : (group + 1) * CH, KVW:]

    def backward(heads):
        query = {h: stacked(qb, h) for h in heads}
        grad = {h: stacked(g, h) for h in heads}
        score = {h: nt(keys[0, :, columns(h)], query[h]) for h in heads}
        grad_probs = {h: nt(values[0, :, columns(h)], grad[h]) for h in heads}
        for h in heads:
            probs = softmax_t(score[h])
            inner = jnp.sum(probs * grad_probs[h], axis=0, keepdims=True)
            grad_scores = (probs * (grad_probs[h] - inner) * SCALE).astype(BF16)
            gs[h] = grad_scores
            key_grads = nn(grad_scores, query[h])
            value_grads = nn(probs.astype(BF16), grad[h])
            own[:, columns(h)] = key_grads[BLK:].astype(BF16)
            own[:, columns(KVH + h)] = value_grads[BLK:].astype(BF16)
            pkg[:, columns(h)] = key_grads[:BLK].astype(BF16)
            pvg[:, columns(h)] = value_grads[:BLK].astype(BF16)

    def forward(heads):
        score = {h: nt(keys[1, :, columns(h)], stacked(qf, h)) for h in heads}
        for h in heads:
            attended = tn(softmax_t(score[h]).astype(BF16), values[1, :, columns(h)])
            for j in range(GROUP):
                at = columns(h * GROUP + j)
                fwd[:, at] = (
                    hid[CH:, at].astype(F32) + attended[j * CH : (j + 1) * CH]
                ).astype(BF16)

    def backed():
        for c in range(CHUNKS):
            at = slice(c * STEP, (c + 1) * STEP)
            back[:, at] = (g[:, at].astype(F32) + nt(own[...], weight[at, :])).astype(BF16)

    def sent():
        for t in range(CHIPS):
            put(own, send_h.at[t, :, pl.ds(ROWS, 2 * KVW)])
        put(pkg, pkg_h)
        put(pvg, pvg_h)
        put(gs, gs_h)
        put(keys.at[0], keys_h)

    project()
    for copy in load[2:]:
        copy.wait()
    backward(range(KVH))
    sent()
    forward(range(KVH))
    put(fwd, fwd_h)
    backed()
    put(back, back_h)
    for copy in out:
        copy.wait()


def query_kernel(gs, keys, out):
    for h in range(KVH):
        grad = tn(gs[h], keys[:, h * HD : (h + 1) * HD])
        for j in range(GROUP):
            cols = slice((h * GROUP + j) * HD, (h * GROUP + j + 1) * HD)
            out[:, cols] = grad[j * CH : (j + 1) * CH].astype(BF16)


def weight_kernel(core, recv, mine, theirs):
    here = core[0]
    grads = recv[:, :, ROWS:].reshape(CHIPS * CH, 2 * KVW)
    low = tn(recv[:, :, :HALF].reshape(CHIPS * CH, HALF), grads)
    high = tn(recv[:, :, HALF:ROWS].reshape(CHIPS * CH, HALF), grads)
    first = here == 0
    mine[...] = jnp.where(first, low, high)
    theirs[...] = jnp.where(first, high, low).astype(BF16)


def sum_kernel(
    core, mine, both, back_in, fwd_in,
    key_out, value_out, back_out, fwd_out,
    key_grad, value_grad, sem,
):
    moves = [
        pltpu.make_async_copy(fwd_in, fwd_out, sem.at[0]),
        pltpu.make_async_copy(back_in, back_out, sem.at[1]),
        pltpu.make_async_copy(key_grad, key_out, sem.at[2]),
        pltpu.make_async_copy(value_grad, value_out, sem.at[3]),
    ]
    for copy in moves[:2]:
        copy.start()
    total = mine[...] + both[1 - core[0]].astype(F32)
    key_grad[...] = total[:, :KVW].astype(BF16)
    value_grad[...] = total[:, KVW:].astype(BF16)
    for copy in moves[2:]:
        copy.start()
    for copy in moves:
        copy.wait()


def call(kernel, outs, scratch, flops, in_specs, out_specs, size=62):
    return pl.pallas_call(
        kernel,
        out_shape=[jax.ShapeDtypeStruct(s, t) for s, t in outs],
        in_specs=in_specs,
        out_specs=out_specs,
        scratch_shapes=scratch,
        compiler_params=pltpu.CompilerParams(vmem_limit_bytes=size * 1024 * 1024),
        cost_estimate=pl.CostEstimate(flops=flops, bytes_accessed=6 << 20, transcendentals=200000),
    )


def spec(space):
    return pl.BlockSpec(memory_space=space)


def section_call(*arrays):
    dma = pltpu.SemaphoreType.DMA
    wide, kv = (CH, D), (KEYS, KVW)
    return call(
        section_kernel,
        [
            ((CHIPS, CH, ROWS + 2 * KVW), BF16),
            (wide, BF16),
            (wide, BF16),
            ((BLK, KVW), BF16),
            ((BLK, KVW), BF16),
            ((KVH, KEYS, GROUP * CH), BF16),
            (kv, BF16),
        ],
        [SMEM((2,), jnp.int32), VMEM((2 * CH, D), BF16)]
        + [VMEM(wide, BF16)] * 3
        + [VMEM((2,) + kv, BF16)] * 2
        + [VMEM((D, 2 * KVW), BF16), VMEM((CH, 2 * KVW), BF16)]
        + [VMEM(wide, BF16)] * 2
        + [VMEM((BLK, KVW), BF16)] * 2
        + [VMEM((KVH, KEYS, GROUP * CH), BF16), dma((10,)), dma((2 * CHUNKS,)), dma((22,))],
        1_600_000_000,
        [spec(ANY)] * 10,
        [spec(ANY)] * 7,
    )(*arrays)


def along(value, axis, steps, wrap):
    count = lax.axis_size(axis)
    pairs = [(i, (i + steps) % count) for i in range(count) if wrap or 0 <= i + steps < count]
    return lax.ppermute(value, axis, pairs)


def per_device(
    fwd_hidden, fwd_query, bwd_hidden, bwd_query, bwd_grad,
    prefix_keys, prefix_values, key_weight, value_weight, block_ids,
):
    count = lax.axis_size("dp")
    dma = pltpu.SemaphoreType.DMA
    wide = (CH, D)
    ids = block_ids.reshape(2)
    send, out_fwd, out_bwd, pkg, pvg, gs, keys_bwd = section_call(
        ids, bwd_hidden[0, 0], fwd_hidden[0, 0], bwd_query[0, 0], fwd_query[0, 0], bwd_grad[0, 0],
        prefix_keys[0, 0], prefix_values[0, 0], key_weight[0], value_weight[0],
    )
    same_core = [[2 * t + c for t in range(count // 2)] for c in range(2)]
    pairs = [[2 * t, 2 * t + 1] for t in range(count // 2)]
    recv = lax.all_to_all(send, "dp", 0, 0, tiled=True, axis_index_groups=same_core)
    prev_grad = along(out_bwd, "section", -1, False)
    next_hidden = along(out_fwd, "section", 1, True)
    (query_grad,) = call(
        query_kernel,
        [(wide, BF16)],
        [],
        100_000_000,
        [spec(VMEM)] * 2,
        [spec(VMEM)],
        16,
    )(gs, keys_bwd)
    core = lax.axis_index("dp") & 1
    mine, theirs = call(
        weight_kernel,
        [((HALF, 2 * KVW), F32), ((HALF, 2 * KVW), BF16)],
        [],
        270_000_000,
        [spec(SMEM), spec(VMEM)],
        [spec(VMEM)] * 2,
        16,
    )(core.reshape(1), recv)
    both = lax.all_gather(theirs, "dp", axis=0, axis_index_groups=pairs)
    key_weight_grad, value_weight_grad, prev_grad, next_hidden = call(
        sum_kernel,
        [((HALF, KVW), BF16)] * 2 + [(wide, BF16)] * 2,
        [VMEM((HALF, KVW), BF16)] * 2 + [dma((4,))],
        1_000_000,
        [spec(SMEM)] + [spec(VMEM)] * 2 + [spec(ANY)] * 2,
        [spec(ANY)] * 4,
        16,
    )(core.reshape(1), mine, both, prev_grad, next_hidden)
    return (
        next_hidden[None, None],
        prev_grad[None, None],
        query_grad[None, None],
        pkg[None, None, None],
        pvg[None, None, None],
        key_weight_grad[None],
        value_weight_grad[None],
    )


def solution(mesh):
    device = P("section", "dp")
    return jax.shard_map(
        per_device,
        mesh=mesh,
        in_specs=(device,) * 7 + (P("section"),) * 2 + (device,),
        out_specs=(device,) * 5 + (P("section", "dp"),) * 2,
        check_vma=False,
    )
```
